32 devices in a mesh: wide: 4 (over z), context: 4 (over x, core), tensor: 2 (over y).
Axes of the slice: x: 2, y: 2, z: 4, core: 2. Of those that a mesh axis runs over, the one named last changes fastest.
Arguments:
- tokens: bfloat16 [12288, 2048], P(('wide', 'context')), may hold values from -6 to 6
- segment_of: int32 [12288], P('wide'), may hold values from 0 to 12, as said below
- parent_of: int32 [52], P('wide'), may hold values from 0 to 12, as said below
- valid: int32 [12288], P('wide'), may hold values from 0 to 1, as said below
- positions: int32 [12288], P(('wide', 'context')), may hold values from 0 to 1279, as said below
- g_attn: bfloat16 [2048], P('wide'), may hold values from 0.25 to 1.75
- w_q: bfloat16 [2048, 2048], P('wide', 'tensor'), may hold values from -0.125 to 0.125
- key_projection: bfloat16 [2048, 1024], P('wide', 'tensor'), may hold values from -0.125 to 0.125
- value_projection: bfloat16 [2048, 1024], P('wide', 'tensor'), may hold values from -0.125 to 0.125
- w_g: bfloat16 [2048, 16], P('wide', 'tensor'), may hold values from -0.125 to 0.125
- q_gain: bfloat16 [128], replicated, may hold values from 0.25 to 1.75
- k_gain: bfloat16 [128], replicated, may hold values from 0.25 to 1.75
- w_o: bfloat16 [2048, 2048], P('tensor', 'wide'), may hold values from -1 to 1
- g_mlp: bfloat16 [2048], P('wide'), may hold values from 0.25 to 1.75
- w_gate: bfloat16 [2048, 6144], P('wide', 'tensor'), may hold values from -0.125 to 0.125
- w_up: bfloat16 [2048, 6144], P('wide', 'tensor'), may hold values from -0.125 to 0.125
- w_down: bfloat16 [6144, 2048], P('tensor', 'wide'), may hold values from -0.078125 to 0.078125
- cotangent: bfloat16 [12288, 2048], P(('wide', 'context')), may hold values from -6 to 6
Outputs:
- layer_out: bfloat16 [12288, 2048], P(('wide', 'context'))
- grad_tokens: float32 [12288, 2048], P(('wide', 'context'))
- grad_g_attn: float32 [2048], P('wide')
- grad_w_q: float32 [2048, 2048], P('wide', 'tensor')
- grad_w_k: float32 [2048, 1024], P('wide', 'tensor')
- grad_w_v: float32 [2048, 1024], P('wide', 'tensor')
- grad_w_g: float32 [2048, 16], P('wide', 'tensor')
- grad_q_gain: float32 [128], replicated
- grad_k_gain: float32 [128], replicated
- grad_w_o: float32 [2048, 2048], P('tensor', 'wide')
- grad_g_mlp: float32 [2048], P('wide')
- grad_w_gate: float32 [2048, 6144], P('wide', 'tensor')
- grad_w_up: float32 [2048, 6144], P('wide', 'tensor')
- grad_w_down: float32 [6144, 2048], P('tensor', 'wide')
The draws below stay inside these ranges and needn't reach their ends.
Inputs may be any that keep to these rules, and one draw needn't show every extreme that they name: `segment_of`: each group of 3072 tokens holds 1 tree and one block of 512 padding tokens. A tree is a trunk of 1024 tokens, 4 branches of 128 tokens, and 2 leaves of 128 tokens for each branch. Every trunk, branch and leaf is a run of consecutive tokens with a number of its own, and it lies after its parent. The segments of different trees and the padding block may lie between one another. In each group, one tree's trunk starts at the group's first token and one of its leaves ends at the group's last. The padding block lies between segments and has number 0. `parent_of`: entry s of a group's 13 entries is the segment that segment s hangs from; a trunk hangs from itself. `valid`: 1 on the trees' tokens, 0 on the padding block. `positions`: A token's place along its root-to-leaf path: trunk tokens count from 0, a branch continues from 1024, a leaf from 1152; padding has 0.
All inputs are finite; a program needn't handle non-finite values.
Results may differ from the reference program's by a relative error of at most 0.02.
Values may be sent and summed in bfloat16 or wider, within the bound.
No kernel may reach another device: no remote copies, remote signals or barrier semaphores. Data moves between devices by JAX's collectives and lax.ppermute only.
A program may use at most 256 MiB of HBM per device.

```python
import jax
import jax.numpy as jnp
from jax import lax

MODEL_WIDTH = 2048
QUERY_HEADS = 16
KEY_VALUE_HEADS = 8
HEAD_SIZE = 128
FF = 6144
TOK_DEV = 768
TRUNK = 1024
SEGLEN = 128
BRANCHES = 4
LEAVES = 2
TREE = 2560
SEG_TREE = 13
GROUP_TOK = 3072
GROUPS = 4
TOKENS = 12288
TREES = 1
SEGS = 13
N_CONTEXT = 4


def group_layout(group_key):
    label_key, score_key, pick_key, pad_key = jax.random.split(group_key, 4)
    unit_count = TREES * SEG_TREE + 1
    score_span = 1 << 20
    slot_all = jnp.arange(SEG_TREE, dtype=jnp.int32)
    branch_number = jnp.maximum(slot_all - 1, 0) // (1 + LEAVES)
    slot_rest = jnp.maximum(slot_all - 1, 0) % (1 + LEAVES)
    slot_local = jnp.where(slot_all == 0, 0, jnp.where(slot_rest == 0, 1 + branch_number, 1 + BRANCHES + branch_number * LEAVES + slot_rest - 1))
    slot_kind = jnp.where(slot_all == 0, 0, jnp.where(slot_rest == 0, 1, 2))
    slot_length = jnp.where(slot_all == 0, TRUNK, SEGLEN)
    raw_scores = jax.random.randint(score_key, (TREES, SEG_TREE), 0, score_span, dtype=jnp.int32) * unit_count + jnp.arange(TREES * SEG_TREE, dtype=jnp.int32).reshape(TREES, SEG_TREE)
    tree_scores = jnp.sort(raw_scores, axis=1)
    chosen = jax.random.randint(pick_key, (), 0, TREES, dtype=jnp.int32)
    tree_index = jnp.arange(TREES, dtype=jnp.int32)[:, None]
    top_score = score_span * unit_count + unit_count
    tree_scores = jnp.where((tree_index == chosen) & (slot_all[None, :] == 0), -2, tree_scores)
    tree_scores = jnp.where((tree_index == chosen) & (slot_all[None, :] == SEG_TREE - 1), top_score, tree_scores)
    pad_score = jax.random.randint(pad_key, (), 0, score_span, dtype=jnp.int32) * unit_count + (unit_count - 1)
    all_scores = jnp.concatenate([tree_scores.reshape(-1), pad_score[None]])
    order = jnp.argsort(all_scores, stable=True).astype(jnp.int32)
    pad_count = GROUP_TOK - TREES * TREE
    unit_length = jnp.concatenate([jnp.tile(slot_length, TREES), jnp.full((1,), pad_count, jnp.int32)])
    unit_tree = jnp.concatenate([jnp.repeat(jnp.arange(TREES, dtype=jnp.int32), SEG_TREE), jnp.zeros((1,), jnp.int32)])
    unit_slot = jnp.concatenate([jnp.tile(slot_all, TREES), jnp.zeros((1,), jnp.int32)])
    sorted_length = unit_length[order]
    ends = jnp.cumsum(sorted_length).astype(jnp.int32)
    row_index = jnp.arange(GROUP_TOK, dtype=jnp.int32)
    which = jnp.searchsorted(ends, row_index, side='right').astype(jnp.int32)
    unit = order[which]
    offset = row_index - (ends[which] - sorted_length[which])
    is_pad = unit == unit_count - 1
    row_tree = unit_tree[unit]
    row_slot = unit_slot[unit]
    kind = slot_kind[row_slot]
    depth = jnp.where(kind == 0, offset, jnp.where(kind == 1, TRUNK + offset, TRUNK + SEGLEN + offset))
    seg_labels = jax.random.permutation(label_key, SEGS).astype(jnp.int32)
    group_seg = row_tree * SEG_TREE + slot_local[row_slot]
    segments = jnp.where(is_pad, 0, seg_labels[group_seg])
    live_rows = jnp.where(is_pad, 0, 1).astype(jnp.int32)
    depths = jnp.where(is_pad, 0, depth).astype(jnp.int32)
    seg_all = jnp.arange(SEGS, dtype=jnp.int32)
    local_all = seg_all % SEG_TREE
    parent_local = jnp.where(local_all <= BRANCHES, 0, 1 + (local_all - 1 - BRANCHES) // LEAVES)
    parent_within = seg_all // SEG_TREE * SEG_TREE + parent_local
    parents = jnp.zeros((SEGS,), jnp.int32).at[seg_labels].set(seg_labels[parent_within])
    return (segments, parents, live_rows, depths)


def tree_layout(key):
    base_key = jax.random.fold_in(key, 101)
    group_keys = jax.random.split(base_key, GROUPS)
    segments, parents, live_rows, depths = jax.vmap(group_layout)(group_keys)
    return (segments.reshape(TOKENS), parents.reshape(GROUPS * SEGS), live_rows.reshape(TOKENS), depths.reshape(TOKENS))


def draw_segment_of(key, part):
    return tree_layout(key)[0]


def draw_parent_of(key, part):
    return tree_layout(key)[1]


def draw_valid(key, part):
    return tree_layout(key)[2]


def draw_positions(key, part):
    return tree_layout(key)[3]


def levels(rng, extent, shards, least, largest):
    def one(dim, parts):
        heights = jax.random.uniform(jax.random.fold_in(jax.random.fold_in(rng, 6), dim), (parts,), jnp.float32, least / len(shards), largest / len(shards))
        return jnp.repeat(jnp.exp(heights), extent[dim] // parts).reshape((-1,) + (1,) * (len(extent) - dim - 1))

    factor_of = one(*shards[0])
    for cut in shards[1:]:
        factor_of = factor_of * one(*cut)
    return factor_of


def centred(key, extent, width, reach, cuts=(), kind=jnp.bfloat16):
    array = width * jax.random.normal(key, extent, jnp.float32)
    if cuts:
        array = array * levels(key, extent, cuts, -0.22, 0.18)
    return jnp.clip(array, -reach, reach).astype(kind)


def setup_inputs(seed: int = 0) -> dict:
    keys = jax.random.split(jax.random.key(seed), 19)
    tokens = centred(keys[0], (TOKENS, MODEL_WIDTH), 1.0, 6.0, ((0, 16),))
    segment_of = draw_segment_of(jax.random.fold_in(keys[18], 71), 0)
    parent_of = draw_parent_of(jax.random.fold_in(keys[18], 71), 0)
    valid = draw_valid(jax.random.fold_in(keys[18], 71), 0)
    positions = draw_positions(jax.random.fold_in(keys[18], 71), 0)
    g_attn = jnp.clip(1.0 + 0.15 * jax.random.normal(keys[5], (MODEL_WIDTH,), jnp.float32), 0.25, 1.75).astype(jnp.bfloat16)
    w_q = centred(keys[6], (MODEL_WIDTH, QUERY_HEADS * HEAD_SIZE), MODEL_WIDTH ** -0.5, 0.125, ((0, 4), (1, 2)))
    key_projection = centred(keys[7], (MODEL_WIDTH, KEY_VALUE_HEADS * HEAD_SIZE), MODEL_WIDTH ** -0.5, 0.125, ((0, 4), (1, 2)))
    value_projection = centred(keys[8], (MODEL_WIDTH, KEY_VALUE_HEADS * HEAD_SIZE), MODEL_WIDTH ** -0.5, 0.125, ((0, 4), (1, 2)))
    w_g = centred(keys[9], (MODEL_WIDTH, QUERY_HEADS), MODEL_WIDTH ** -0.5, 0.125, ((0, 4), (1, 2)))
    q_gain = jnp.clip(1.0 + 0.15 * jax.random.normal(keys[10], (HEAD_SIZE,), jnp.float32), 0.25, 1.75).astype(jnp.bfloat16)
    k_gain = jnp.clip(1.0 + 0.15 * jax.random.normal(keys[11], (HEAD_SIZE,), jnp.float32), 0.25, 1.75).astype(jnp.bfloat16)
    w_o = centred(keys[12], (QUERY_HEADS * HEAD_SIZE, MODEL_WIDTH), (QUERY_HEADS * HEAD_SIZE // 64) ** -0.5, 1.0, ((0, 2), (1, 4)))
    g_mlp = jnp.clip(1.0 + 0.15 * jax.random.normal(keys[13], (MODEL_WIDTH,), jnp.float32), 0.25, 1.75).astype(jnp.bfloat16)
    w_gate = centred(keys[14], (MODEL_WIDTH, FF), MODEL_WIDTH ** -0.5, 0.125, ((0, 4), (1, 2)))
    w_up = centred(keys[15], (MODEL_WIDTH, FF), MODEL_WIDTH ** -0.5, 0.125, ((0, 4), (1, 2)))
    w_down = centred(keys[16], (FF, MODEL_WIDTH), FF ** -0.5, 0.078125, ((0, 2), (1, 4)))
    cotangent = centred(keys[17], (TOKENS, MODEL_WIDTH), 1.0, 6.0, ((0, 16),))
    return dict(tokens=tokens, segment_of=segment_of, parent_of=parent_of, valid=valid, positions=positions, g_attn=g_attn, w_q=w_q, key_projection=key_projection, value_projection=value_projection, w_g=w_g, q_gain=q_gain, k_gain=k_gain, w_o=w_o, g_mlp=g_mlp, w_gate=w_gate, w_up=w_up, w_down=w_down, cotangent=cotangent)


@jax.custom_vjp
def low(v):
    return lax.optimization_barrier(v.astype(jnp.bfloat16)).astype(jnp.float32)

@jax.custom_vjp
def low_back(v):
    return v

def low_keep(v):
    return (low(v), None)

def low_pass(kept, grad):
    return (grad,)

def back_keep(v):
    return (v, None)

def back_low(kept, grad):
    return (low(grad),)
low.defvjp(low_keep, low_pass)
low_back.defvjp(back_keep, back_low)
EPSILON = 1e-06
ROPE_BASE = 1000000.0

def product(left, right):
    return jnp.dot(left, right, precision=lax.Precision.HIGHEST, preferred_element_type=jnp.float32)

def rms_scale(values, gain):
    return values * lax.rsqrt(lax.optimization_barrier(jnp.mean(values * values, axis=-1, keepdims=True)) + EPSILON) * gain

def rope_tables(positions, head_width):
    half_width = head_width // 2
    frequency = ROPE_BASE ** (-(jnp.arange(half_width, dtype=jnp.float32) * 2.0 / head_width))
    angles = positions.astype(jnp.float32)[:, None] * frequency[None, :]
    cosine_table = jnp.concatenate([jnp.cos(angles), jnp.cos(angles)], axis=-1)
    sine_table = jnp.concatenate([jnp.sin(angles), jnp.sin(angles)], axis=-1)
    return (cosine_table, sine_table)

def rotate(values, cosine_table, sine_table):
    half_width = values.shape[-1] // 2
    turned = jnp.concatenate([-values[..., half_width:], values[..., :half_width]], axis=-1)
    return values * cosine_table[:, None, :] + turned * sine_table[:, None, :]

def head_prep(linear, gain, cosine_table, sine_table):
    heads = linear.reshape(linear.shape[0], -1, gain.shape[0])
    return rotate(rms_scale(heads, gain), cosine_table, sine_table)

def ancestry(parent_group):
    seg_count = parent_group.shape[0]
    seg_index = jnp.arange(seg_count, dtype=jnp.int32)
    single = (parent_group[:, None] == seg_index[None, :]).astype(jnp.float32)
    lookup_table = jnp.eye(seg_count, dtype=jnp.float32) + single + product(single, single)
    return jnp.minimum(lookup_table, 1.0)

def attention_output(rotary_queries, rotary_keys, value_lowered, segment_grouping, lookup_table, group_alive_mask):
    rows_per_group = rotary_queries.shape[0]
    rows_per_block = min(512, rows_per_group)
    count_of_blocks = rows_per_group // rows_per_block
    head_repeat = QUERY_HEADS // KEY_VALUE_HEADS
    query_matrix = rotary_queries.reshape(count_of_blocks, rows_per_block, KEY_VALUE_HEADS, head_repeat, HEAD_SIZE)
    key_index = jnp.arange(rows_per_group, dtype=jnp.int32)
    key_live = group_alive_mask > 0

    def block_fn(pieces):
        q_block, first_row = pieces
        query_index = first_row + jnp.arange(rows_per_block, dtype=jnp.int32)
        query_seg = lax.dynamic_slice_in_dim(segment_grouping, first_row, rows_per_block)
        query_live = lax.dynamic_slice_in_dim(key_live, first_row, rows_per_block)
        on_path = jnp.take(lookup_table[query_seg], segment_grouping, axis=1) > 0.5
        earlier = key_index[None, :] < query_index[:, None]
        diagonal = key_index[None, :] == query_index[:, None]
        allowed = on_path & earlier & query_live[:, None] & key_live[None, :] | diagonal
        scores = jnp.einsum('qgrd,kgd->qgrk', q_block, rotary_keys, precision=lax.Precision.HIGHEST) * HEAD_SIZE ** (-0.5)
        scores = low_back(scores)
        scores = jnp.where(allowed[:, None, None, :], scores, -1e+30)
        row_max = lax.optimization_barrier(jnp.max(scores, axis=-1, keepdims=True))
        weights = jnp.exp(scores - row_max)
        probs = weights / lax.optimization_barrier(jnp.sum(weights, axis=-1, keepdims=True))
        return jnp.einsum('qgrk,kgd->qgrd', low(probs), value_lowered, precision=lax.Precision.HIGHEST)
    firsts = jnp.arange(count_of_blocks, dtype=jnp.int32) * rows_per_block
    result = lax.map(jax.checkpoint(block_fn), (query_matrix, firsts))
    return result.reshape(rows_per_group, QUERY_HEADS, HEAD_SIZE)

def layer(params, tokens_f, segment_grouping, lookup_table, group_alive_mask, pos_group):
    g_attn, w_q, key_projection, value_projection, w_g, q_gain, k_gain, w_o, g_mlp, w_gate, w_up, w_down = params
    rows_per_group = tokens_f.shape[0]
    cosine_table, sine_table = rope_tables(pos_group, HEAD_SIZE)
    normed = low(rms_scale(tokens_f, g_attn))
    query_proj = low_back(product(normed, w_q))
    key_proj = low_back(product(normed, key_projection))
    value_lowered = low(low_back(product(normed, value_projection)))
    gate_proj = low_back(product(normed, w_g))
    rotary_queries = low(head_prep(query_proj, q_gain, cosine_table, sine_table))
    rotary_keys = low(head_prep(key_proj, k_gain, cosine_table, sine_table))
    attended_rows = low_back(attention_output(rotary_queries, rotary_keys, value_lowered.reshape(rows_per_group, KEY_VALUE_HEADS, HEAD_SIZE), segment_grouping, lookup_table, group_alive_mask))
    gated = low((attended_rows * jax.nn.sigmoid(gate_proj)[:, :, None]).reshape(rows_per_group, QUERY_HEADS * HEAD_SIZE))
    middle = tokens_f + low_back(product(gated, w_o))
    normed_mlp = low(rms_scale(middle, g_mlp))
    gate_mlp = low_back(product(normed_mlp, w_gate))
    up_mlp = low_back(product(normed_mlp, w_up))
    mixed = low(jax.nn.silu(gate_mlp) * up_mlp)
    return middle + low_back(product(mixed, w_down))

def reference(tokens, segment_of, parent_of, valid, positions, g_attn, w_q, key_projection, value_projection, w_g, q_gain, k_gain, w_o, g_mlp, w_gate, w_up, w_down, cotangent):
    params = tuple((weight.astype(jnp.float32) for weight in (g_attn, w_q, key_projection, value_projection, w_g, q_gain, k_gain, w_o, g_mlp, w_gate, w_up, w_down)))
    rows_per_group = TOK_DEV * N_CONTEXT
    stacked = (tokens.astype(jnp.float32).reshape(GROUPS, rows_per_group, MODEL_WIDTH), segment_of.reshape(GROUPS, rows_per_group), parent_of.reshape(GROUPS, SEGS), valid.reshape(GROUPS, rows_per_group), positions.reshape(GROUPS, rows_per_group), cotangent.astype(jnp.float32).reshape(GROUPS, rows_per_group, MODEL_WIDTH))

    def one_group(running, pieces):
        tokens_f, segment_grouping, parent_group, group_alive_mask, pos_group, cot_group = pieces
        lookup_table = ancestry(parent_group)

        def forward(weights, values):
            return layer(weights, values, segment_grouping, lookup_table, group_alive_mask, pos_group)
        output, pullback = jax.vjp(forward, params, tokens_f)
        weight_grads, token_grads = pullback(cot_group)
        running = jax.tree.map(lambda left, right: left + right, running, weight_grads)
        return (running, (output.astype(jnp.bfloat16), token_grads))
    initial = jax.tree.map(jnp.zeros_like, params)
    totals, (outputs, token_grads) = lax.scan(one_group, initial, stacked)
    return (outputs.reshape(TOKENS, MODEL_WIDTH), token_grads.reshape(TOKENS, MODEL_WIDTH), totals[0], totals[1], totals[2], totals[3], totals[4], totals[5], totals[6], totals[7], totals[8], totals[9], totals[10], totals[11])
```

```python
import functools

import jax
import jax.numpy as jnp
from jax import lax
from jax.experimental import pallas as pl
from jax.experimental.pallas import tpu as pltpu
from jax.sharding import PartitionSpec as P

EPSILON = 1e-06
ROPE_BASE = 1000000.0


def product(left, right):
    return jnp.dot(left, right, preferred_element_type=jnp.float32)


def product_left(left, right):
    return lax.dot_general(
        left, right, (((0,), (0,)), ((), ())), preferred_element_type=jnp.float32
    )


def product_right(left, right):
    return lax.dot_general(
        left, right, (((1,), (1,)), ((), ())), preferred_element_type=jnp.float32
    )


def rms_scale(values, gain):
    return values * lax.rsqrt(jnp.mean(values * values, axis=-1, keepdims=True) + EPSILON) * gain


def rope_tables(positions, head_width):
    half_width = head_width // 2
    frequency = ROPE_BASE ** (-(jnp.arange(half_width, dtype=jnp.float32) * 2.0 / head_width))
    angles = positions.astype(jnp.float32)[:, None] * frequency[None, :]
    cosine_table = jnp.concatenate([jnp.cos(angles), jnp.cos(angles)], axis=-1)
    sine_table = jnp.concatenate([jnp.sin(angles), jnp.sin(angles)], axis=-1)
    return (cosine_table, sine_table)


def rotate(values, cosine_table, sine_table):
    half_width = values.shape[-1] // 2
    turned = jnp.concatenate([-values[..., half_width:], values[..., :half_width]], axis=-1)
    return values * cosine_table[:, None, :] + turned * sine_table[:, None, :]


def head_prep(linear, gain, cosine_table, sine_table):
    heads = linear.reshape(linear.shape[0], -1, gain.shape[0])
    return rotate(rms_scale(heads, gain), cosine_table, sine_table)


def norm_backward(values, gain, incoming):
    norm_value, norm_pull = jax.vjp(rms_scale, values, gain)
    return norm_pull(incoming)


def path_mask(tree_rows, key_rows, first_row, key_count):
    rows_per_block = tree_rows.shape[0]
    on_path = product_right(tree_rows, key_rows) > 0.5
    query_index = first_row + jnp.arange(rows_per_block, dtype=jnp.int32)
    key_index = jnp.arange(key_count, dtype=jnp.int32)
    earlier = key_index[None, :] < query_index[:, None]
    diagonal = key_index[None, :] == query_index[:, None]
    return on_path & earlier | diagonal


def block_scores(q_block, key_head, allowed, scale):
    scores = (
        jnp.einsum("qrd,kd->qrk", q_block, key_head, preferred_element_type=jnp.float32) * scale
    )
    return jnp.where(allowed[:, None, :], scores, -1e30)


def attend_forward(q_block, key_head, value_head, allowed, scale):
    scores = block_scores(q_block, key_head, allowed, scale)
    row_max = jnp.max(scores, axis=-1, keepdims=True)
    weights = jnp.exp(scores - row_max)
    row_sum = jnp.sum(weights, axis=-1, keepdims=True)
    probs = (weights / row_sum).astype(jnp.bfloat16)
    result = jnp.einsum("qrk,kd->qrd", probs, value_head, preferred_element_type=jnp.float32)
    return (result, (row_max + jnp.log(row_sum))[..., 0])


def attend_backward(q_block, key_head, value_head, grad_block, log_sum, allowed, scale):
    scores = block_scores(q_block, key_head, allowed, scale)
    probs = jnp.exp(scores - log_sum[..., None])
    grad_probs = jnp.einsum(
        "qrd,kd->qrk", grad_block, value_head, preferred_element_type=jnp.float32
    )
    inner = jnp.sum(probs * grad_probs, axis=-1, keepdims=True)
    grad_scores = (probs * (grad_probs - inner)).astype(jnp.bfloat16)
    grad_query = (
        jnp.einsum("qrk,kd->qrd", grad_scores, key_head, preferred_element_type=jnp.float32) * scale
    )
    grad_key = (
        jnp.einsum("qrk,qrd->kd", grad_scores, q_block, preferred_element_type=jnp.float32) * scale
    )
    grad_value = jnp.einsum(
        "qrk,qrd->kd", probs.astype(jnp.bfloat16), grad_block, preferred_element_type=jnp.float32
    )
    return (grad_query, grad_key, grad_value)


def shards(
    tokens,
    segment_of,
    parent_of,
    valid,
    positions,
    g_attn,
    w_q,
    key_projection,
    value_projection,
    w_g,
    q_gain,
    k_gain,
    w_o,
    g_mlp,
    w_gate,
    w_up,
    w_down,
    cotangent,
):
    row_count = tokens.shape[0]
    head_width = q_gain.shape[0]
    rows_per_group = segment_of.shape[0]
    seg_count = parent_of.shape[0]
    scale = head_width ** (-0.5)
    share_rows = row_count // lax.axis_size("tensor")
    share_first = lax.axis_index("tensor") * share_rows
    query_weight, key_weight, value_weight, gate_weight, attn_gain, out_weight = (
        lax.all_gather(w_q, "wide", axis=0, tiled=True),
        lax.all_gather(key_projection, "wide", axis=0, tiled=True),
        lax.all_gather(value_projection, "wide", axis=0, tiled=True),
        lax.all_gather(w_g, "wide", axis=0, tiled=True),
        lax.all_gather(g_attn, "wide", axis=0, tiled=True),
        lax.all_gather(w_o, "wide", axis=1, tiled=True),
    )
    gate_mlp_weight, up_weight, mlp_gain, down_weight = (
        lax.all_gather(w_gate, "wide", axis=0, tiled=True),
        lax.all_gather(w_up, "wide", axis=0, tiled=True),
        lax.all_gather(g_mlp, "wide", axis=0, tiled=True),
        lax.all_gather(w_down, "wide", axis=1, tiled=True),
    )
    tokens_f = tokens.astype(jnp.float32)
    tokens_share = lax.dynamic_slice_in_dim(tokens_f, share_first, share_rows)
    attn_gain_f = attn_gain.astype(jnp.float32)
    mlp_gain_f = mlp_gain.astype(jnp.float32)
    query_gain = q_gain.astype(jnp.float32)
    key_gain = k_gain.astype(jnp.float32)
    cosine_table, sine_table = rope_tables(positions, head_width)
    normed = rms_scale(tokens_f, attn_gain_f).astype(jnp.bfloat16)
    query_proj = product(normed, query_weight)
    key_proj = product(normed, key_weight)
    value_proj = product(normed, value_weight)
    gate_proj = product(normed, gate_weight)
    query_rot = head_prep(query_proj, query_gain, cosine_table, sine_table).astype(jnp.bfloat16)
    key_rot = head_prep(key_proj, key_gain, cosine_table, sine_table).astype(jnp.bfloat16)
    head_count = query_rot.shape[1]
    kv_count = key_rot.shape[1]
    head_repeat = head_count // kv_count
    keys_all, values_all = (
        lax.all_gather(
            key_rot.reshape(row_count, kv_count * head_width), "context", axis=0, tiled=True
        ),
        lax.all_gather(value_proj.astype(jnp.bfloat16), "context", axis=0, tiled=True),
    )
    seg_index = jnp.arange(seg_count, dtype=jnp.int32)
    single = (parent_of[:, None] == seg_index[None, :]).astype(jnp.float32)
    lookup_table = jnp.minimum(
        jnp.eye(seg_count, dtype=jnp.float32) + single + product(single, single), 1.0
    )
    live_all = valid.astype(jnp.float32)
    key_rows = (segment_of[:, None] == seg_index[None, :]).astype(jnp.float32) * live_all[:, None]
    own_first = lax.axis_index("context") * row_count
    own_seg = lax.dynamic_slice_in_dim(segment_of, own_first, row_count)
    own_live = lax.dynamic_slice_in_dim(live_all, own_first, row_count)
    tree_rows = (
        product((own_seg[:, None] == seg_index[None, :]).astype(jnp.float32), lookup_table)
        * own_live[:, None]
    )
    rows_per_block = min(256, row_count)
    count_of_blocks = row_count // rows_per_block
    tree_blocks = tree_rows.reshape(count_of_blocks, rows_per_block, seg_count)
    block_firsts = own_first + jnp.arange(count_of_blocks, dtype=jnp.int32) * rows_per_block
    query_heads = query_rot.reshape(
        count_of_blocks, rows_per_block, kv_count, head_repeat, head_width
    ).transpose(2, 0, 1, 3, 4)
    key_heads = keys_all.reshape(rows_per_group, kv_count, head_width).transpose(1, 0, 2)
    value_heads = values_all.reshape(rows_per_group, kv_count, head_width).transpose(1, 0, 2)

    def head_forward(pieces):
        query_head, key_head, value_head = pieces

        def block_forward(block_pieces):
            q_block, tree_block, first_row = block_pieces
            allowed = path_mask(tree_block, key_rows, first_row, rows_per_group)
            return attend_forward(q_block, key_head, value_head, allowed, scale)

        return lax.map(block_forward, (query_head, tree_blocks, block_firsts))

    attended_heads, log_sums = lax.map(head_forward, (query_heads, key_heads, value_heads))
    attended_rows = attended_heads.transpose(1, 2, 0, 3, 4).reshape(
        row_count, head_count, head_width
    )
    gate_sig = jax.nn.sigmoid(gate_proj)
    gated = (
        (attended_rows * gate_sig[:, :, None])
        .reshape(row_count, head_count * head_width)
        .astype(jnp.bfloat16)
    )
    attn_terms = product(gated, out_weight)
    middle = tokens_f + lax.psum(attn_terms, "tensor")
    middle_share = lax.dynamic_slice_in_dim(middle, share_first, share_rows)
    normed_mlp = rms_scale(middle, mlp_gain_f).astype(jnp.bfloat16)
    gate_mlp = product(normed_mlp, gate_mlp_weight)
    up_mlp = product(normed_mlp, up_weight)
    mixed = (jax.nn.silu(gate_mlp) * up_mlp).astype(jnp.bfloat16)
    mlp_terms = product(mixed, down_weight)
    layer_out = (
        middle + lax.psum(mlp_terms.astype(jnp.bfloat16), "tensor").astype(jnp.float32)
    ).astype(jnp.bfloat16)
    grad_down = product_left(mixed, cotangent)
    grad_mixed = product_right(cotangent, down_weight)
    sig_mlp = jax.nn.sigmoid(gate_mlp)
    grad_gate_low = (grad_mixed * up_mlp * sig_mlp * (1.0 + gate_mlp * (1.0 - sig_mlp))).astype(
        jnp.bfloat16
    )
    grad_up_low = (grad_mixed * gate_mlp * sig_mlp).astype(jnp.bfloat16)
    grad_gate_w = product_left(normed_mlp, grad_gate_low)
    grad_up_w = product_left(normed_mlp, grad_up_low)
    grad_normed_share = lax.psum_scatter(
        product_right(grad_gate_low, gate_mlp_weight) + product_right(grad_up_low, up_weight),
        "tensor",
        scatter_dimension=0,
        tiled=True,
    )
    grad_middle_norm, grad_mlp_gain = norm_backward(middle_share, mlp_gain_f, grad_normed_share)
    cot_share = lax.dynamic_slice_in_dim(cotangent, share_first, share_rows).astype(jnp.float32)
    grad_middle_share = cot_share + grad_middle_norm
    grad_attn_share = grad_middle_share.astype(jnp.bfloat16)
    grad_attn_low = lax.all_gather(grad_attn_share, "tensor", axis=0, tiled=True)
    grad_out_w = product_left(gated, grad_attn_low)
    grad_gated = product_right(grad_attn_low, out_weight).reshape(row_count, head_count, head_width)
    grad_attended = (grad_gated * gate_sig[:, :, None]).astype(jnp.bfloat16)
    grad_head_gate = (
        jnp.sum(grad_gated * attended_rows, axis=-1) * gate_sig * (1.0 - gate_sig)
    ).astype(jnp.bfloat16)
    grad_heads = grad_attended.reshape(
        count_of_blocks, rows_per_block, kv_count, head_repeat, head_width
    ).transpose(2, 0, 1, 3, 4)

    def head_backward(pieces):
        query_head, key_head, value_head, grad_head, log_head = pieces

        def block_backward(running, block_pieces):
            q_block, grad_block, log_block, tree_block, first_row = block_pieces
            allowed = path_mask(tree_block, key_rows, first_row, rows_per_group)
            grad_query, grad_key, grad_value = attend_backward(
                q_block, key_head, value_head, grad_block, log_block, allowed, scale
            )
            return ((running[0] + grad_key, running[1] + grad_value), grad_query)

        empty_sum = jnp.zeros((rows_per_group, head_width), jnp.float32)
        key_value_sums, grad_queries = lax.scan(
            block_backward,
            (empty_sum, empty_sum),
            (query_head, grad_head, log_head, tree_blocks, block_firsts),
        )
        return (grad_queries, key_value_sums[0], key_value_sums[1])

    grad_query_heads, grad_key_heads, grad_value_heads = lax.map(
        head_backward, (query_heads, key_heads, value_heads, grad_heads, log_sums)
    )
    grad_keys_all = grad_key_heads.transpose(1, 0, 2).reshape(rows_per_group, kv_count * head_width)
    grad_values_all = grad_value_heads.transpose(1, 0, 2).reshape(
        rows_per_group, kv_count * head_width
    )
    grad_keys, grad_values = (
        lax.psum_scatter(
            grad_keys_all.astype(jnp.bfloat16), "context", scatter_dimension=0, tiled=True
        ).astype(jnp.float32),
        lax.psum_scatter(
            grad_values_all.astype(jnp.bfloat16), "context", scatter_dimension=0, tiled=True
        ).astype(jnp.float32),
    )
    grad_query_rot = grad_query_heads.transpose(1, 2, 0, 3, 4).reshape(
        row_count, head_count, head_width
    )

    def rope_piece(linear, gain):
        return head_prep(linear, gain, cosine_table, sine_table)

    query_value, query_pull = jax.vjp(rope_piece, query_proj, query_gain)
    grad_query_proj, grad_query_gain = query_pull(grad_query_rot)
    key_value, key_pull = jax.vjp(rope_piece, key_proj, key_gain)
    grad_key_proj, grad_key_gain = key_pull(grad_keys.reshape(row_count, kv_count, head_width))
    grad_query_low = grad_query_proj.astype(jnp.bfloat16)
    grad_key_low = grad_key_proj.astype(jnp.bfloat16)
    grad_value_low = grad_values.astype(jnp.bfloat16)
    grad_query_w = product_left(normed, grad_query_low)
    grad_key_w = product_left(normed, grad_key_low)
    grad_value_w = product_left(normed, grad_value_low)
    grad_head_gate_w = product_left(normed, grad_head_gate)
    grad_normed_attn = lax.psum_scatter(
        (
            product_right(grad_query_low, query_weight)
            + product_right(grad_key_low, key_weight)
            + product_right(grad_value_low, value_weight)
            + product_right(grad_head_gate, gate_weight)
        ).astype(jnp.bfloat16),
        "tensor",
        scatter_dimension=0,
        tiled=True,
    ).astype(jnp.float32)
    grad_tokens_norm, grad_attn_gain = norm_backward(tokens_share, attn_gain_f, grad_normed_attn)
    grad_tokens = lax.all_gather(
        (grad_middle_share + grad_tokens_norm).astype(jnp.bfloat16), "tensor", axis=0, tiled=True
    ).astype(jnp.float32)
    sum_query_gain, sum_key_gain, sum_attn_gain, sum_mlp_gain = lax.psum(
        (grad_query_gain, grad_key_gain, grad_attn_gain, grad_mlp_gain),
        ("wide", "context", "tensor"),
    )
    gain_piece = sum_attn_gain.shape[0] // lax.axis_size("wide")
    gain_first = lax.axis_index("wide") * gain_piece
    final_attn_gain = lax.dynamic_slice_in_dim(sum_attn_gain, gain_first, gain_piece)
    final_mlp_gain = lax.dynamic_slice_in_dim(sum_mlp_gain, gain_first, gain_piece)
    (
        share_query,
        share_key,
        share_value,
        share_head_gate,
        share_out,
        share_gate,
        share_up,
        share_down,
    ) = (
        lax.psum_scatter(
            grad_query_w.astype(jnp.bfloat16), "wide", scatter_dimension=0, tiled=True
        ).astype(jnp.float32),
        lax.psum_scatter(
            grad_key_w.astype(jnp.bfloat16), "wide", scatter_dimension=0, tiled=True
        ).astype(jnp.float32),
        lax.psum_scatter(
            grad_value_w.astype(jnp.bfloat16), "wide", scatter_dimension=0, tiled=True
        ).astype(jnp.float32),
        lax.psum_scatter(
            grad_head_gate_w.astype(jnp.bfloat16), "wide", scatter_dimension=0, tiled=True
        ).astype(jnp.float32),
        lax.psum_scatter(
            grad_out_w.astype(jnp.bfloat16), "wide", scatter_dimension=1, tiled=True
        ).astype(jnp.float32),
        lax.psum_scatter(
            grad_gate_w.astype(jnp.bfloat16), "wide", scatter_dimension=0, tiled=True
        ).astype(jnp.float32),
        lax.psum_scatter(
            grad_up_w.astype(jnp.bfloat16), "wide", scatter_dimension=0, tiled=True
        ).astype(jnp.float32),
        lax.psum_scatter(
            grad_down.astype(jnp.bfloat16), "wide", scatter_dimension=1, tiled=True
        ).astype(jnp.float32),
    )
    (
        final_query,
        final_key,
        final_value,
        final_head_gate,
        final_out,
        final_gate,
        final_up,
        final_down,
    ) = (
        lax.psum(share_query.astype(jnp.bfloat16), "context").astype(jnp.float32),
        lax.psum(share_key.astype(jnp.bfloat16), "context").astype(jnp.float32),
        lax.psum(share_value.astype(jnp.bfloat16), "context").astype(jnp.float32),
        lax.psum(share_head_gate.astype(jnp.bfloat16), "context").astype(jnp.float32),
        lax.psum(share_out.astype(jnp.bfloat16), "context").astype(jnp.float32),
        lax.psum(share_gate.astype(jnp.bfloat16), "context").astype(jnp.float32),
        lax.psum(share_up.astype(jnp.bfloat16), "context").astype(jnp.float32),
        lax.psum(share_down.astype(jnp.bfloat16), "context").astype(jnp.float32),
    )
    return (
        layer_out,
        grad_tokens,
        final_attn_gain,
        final_query,
        final_key,
        final_value,
        final_head_gate,
        sum_query_gain,
        sum_key_gain,
        final_out,
        final_mlp_gain,
        final_gate,
        final_up,
        final_down,
    )


BLOCK = 128
TRUNK = 1024
VMEM_BYTES = 62 * 1024 * 1024
X_SWAP = [(0, 2), (2, 0), (1, 3), (3, 1)]
CORE_SWAP = [(0, 1), (1, 0), (2, 3), (3, 2)]
LOW = jnp.bfloat16
F32 = jnp.float32


def over_x(v):
    return lax.ppermute(v, "context", X_SWAP)


def over_core(v):
    return lax.ppermute(v, "context", CORE_SWAP)


def over_y(v):
    return lax.ppermute(v, "tensor", [(0, 1), (1, 0)])


def after(value, *others):
    return lax.optimization_barrier((value,) + others)[0]


def call(body, grid, ins, outs, flops, scratch=(), name=None):
    in_specs, operands = [], []
    for array, block, where in ins:
        operands.append(array)
        if block is None:
            in_specs.append(pl.BlockSpec(memory_space=where))
        elif where is None:
            zero = (0,) * array.ndim
            in_specs.append(
                pl.BlockSpec(block, lambda *_, zero=zero: zero, pipeline_mode=pl.Buffered(1))
            )
        else:
            in_specs.append(pl.BlockSpec(block, where))
    out_specs, out_shape = [], []
    for shape, kind, block, where in outs:
        out_shape.append(jax.ShapeDtypeStruct(shape, kind))
        if block is None:
            out_specs.append(pl.BlockSpec(memory_space=where))
        else:
            out_specs.append(pl.BlockSpec(block, where))
    moved = sum(a.size * a.dtype.itemsize for a in operands)
    moved += sum(s.size * s.dtype.itemsize for s in out_shape)
    return pl.pallas_call(
        body,
        grid=grid,
        in_specs=in_specs,
        out_specs=out_specs,
        out_shape=out_shape,
        scratch_shapes=list(scratch),
        compiler_params=pltpu.CompilerParams(
            vmem_limit_bytes=VMEM_BYTES, dimension_semantics=("arbitrary",) * len(grid)
        ),
        cost_estimate=pl.CostEstimate(flops=flops, bytes_accessed=moved, transcendentals=0),
        name=name,
    )(*operands)


def mm(a, b):
    return lax.dot_general(a, b, (((1,), (0,)), ((), ())), preferred_element_type=F32)


def mm_t(a, b):
    return lax.dot_general(a, b, (((1,), (1,)), ((), ())), preferred_element_type=F32)


def prep_kernel(tok, gain, w_own, w_sis, w_gates, cos, sin, qg, kg, h_out, lin_own, lin_sis, pk_own, pk_sis):
    t = tok[...].astype(F32)
    h = (t * lax.rsqrt(jnp.mean(t * t, -1, keepdims=True) + EPSILON) * gain[...]).astype(LOW)
    h_out[...] = h
    logits = mm_t(h, w_gates[...])
    high = logits.astype(LOW)
    rest = (logits - high.astype(F32)).astype(LOW)
    lane = lax.broadcasted_iota(jnp.int32, logits.shape, 1)
    packed = jnp.where((lane & 2) == 0, high, rest)
    c, s = cos[...], sin[...]
    for w, lin, pk in ((w_own, lin_own, pk_own), (w_sis, lin_sis, pk_sis)):
        u = mm(h, w[...])
        lin[...] = u[:, : 3 * BLOCK]
        for a in range(3):
            head = u[:, a * BLOCK : (a + 1) * BLOCK]
            g = (qg if a < 2 else kg)[...]
            n = head * lax.rsqrt(jnp.mean(head * head, -1, keepdims=True) + EPSILON) * g
            pk[:, a * BLOCK : (a + 1) * BLOCK] = (n * c + pltpu.roll(n, BLOCK // 2, 1) * s).astype(LOW)
        pk[:, 3 * BLOCK : 4 * BLOCK] = u[:, 3 * BLOCK :].astype(LOW)
        pk[:, 4 * BLOCK :] = packed


def locate(tab, block):
    return tab[0, block], pl.multiple_of(tab[1, block], BLOCK)


def gate_column(buf, slot, row):
    lanes = buf[slot, pl.ds(row, BLOCK), 4 * BLOCK :].astype(F32)
    logits = []
    for a in range(2):
        own = lanes[:, a : a + 1] + lanes[:, a + 2 : a + 3]
        sis = lanes[:, a + 4 : a + 5] + lanes[:, a + 6 : a + 7]
        logits.append(jnp.where(slot == 0, own, sis))
    return jax.nn.sigmoid(jnp.concatenate(logits, axis=0))


def stack_heads(block):
    return jnp.concatenate([block[:, :BLOCK], block[:, BLOCK:]], axis=0)


def key_pieces(tab, i, pieces):
    rows = 2 * BLOCK
    out = []
    for first, count in pieces:
        slot, row = locate(tab, first)
        limit = tab[2, i] - first * BLOCK

        def keep(p, limit=limit, size=count * BLOCK):
            col = lax.broadcasted_iota(jnp.int32, (rows, size), 1)
            return jnp.where(col < limit, p, 0.0)

        out.append((slot, row, count * BLOCK, keep))

    def keep_parent(p):
        return jnp.where(tab[5, i] > 0, p, 0.0)

    def keep_own(p):
        col = lax.broadcasted_iota(jnp.int32, (rows, BLOCK), 1)
        row = lax.broadcasted_iota(jnp.int32, (rows, BLOCK), 0) & (BLOCK - 1)
        return jnp.where(((col < row) & (tab[6, i] > 0)) | (col == row), p, 0.0)

    out.append((tab[3, i], pl.multiple_of(tab[4, i], BLOCK), BLOCK, keep_parent))
    slot, row = locate(tab, i)
    out.append((slot, row, BLOCK, keep_own))
    return out


def attend_kernel(blocks, pieces, factor, tab, pk_own, pk_sis, out_own, out_sis, buf, held, sem):
    copies = [
        pltpu.make_async_copy(pk_own, buf.at[0], sem.at[0]),
        pltpu.make_async_copy(pk_sis, buf.at[1], sem.at[1]),
    ]
    for cp in copies:
        cp.start()
    for cp in copies:
        cp.wait()

    def step(i, carry):
        slot, row = locate(tab, i)
        q = stack_heads(buf[slot, pl.ds(row, BLOCK), : 2 * BLOCK])
        total = jnp.zeros((2 * BLOCK, 1), F32)
        acc = jnp.zeros((2 * BLOCK, BLOCK), F32)
        for ks, kr, size, keep in key_pieces(tab, i, pieces):
            key = buf[ks, pl.ds(kr, size), 2 * BLOCK : 3 * BLOCK]
            val = buf[ks, pl.ds(kr, size), 3 * BLOCK : 4 * BLOCK]
            p = keep(jnp.exp2(mm_t(q, key) * factor))
            total = total + jnp.sum(p, axis=-1, keepdims=True)
            acc = acc + mm(p.astype(LOW), val)
        gated = (acc * (gate_column(buf, slot, row) / total)).astype(LOW)
        held[slot, pl.ds(row, BLOCK), :BLOCK] = gated[:BLOCK]
        held[slot, pl.ds(row, BLOCK), BLOCK:] = gated[BLOCK:]
        return carry

    lax.fori_loop(0, blocks, step, 0)
    copies = [
        pltpu.make_async_copy(held.at[0], out_own, sem.at[0]),
        pltpu.make_async_copy(held.at[1], out_sis, sem.at[1]),
    ]
    for cp in copies:
        cp.start()
    for cp in copies:
        cp.wait()


def attend_back_kernel(blocks, pieces, factor, scale, tab, *refs):
    pk_own, pk_sis, ga_own, ga_sis, dg_own, dg_sis, out_own, out_sis, buf, ga, dg, held, dk, dv, sem = refs
    copies = [
        pltpu.make_async_copy(src, dst, sem.at[n])
        for n, (src, dst) in enumerate(
            [
                (pk_own, buf.at[0]),
                (pk_sis, buf.at[1]),
                (ga_own, ga.at[0]),
                (ga_sis, ga.at[1]),
                (dg_own, dg.at[0]),
                (dg_sis, dg.at[1]),
            ]
        )
    ]
    for cp in copies:
        cp.start()
    dk[...] = jnp.zeros_like(dk)
    dv[...] = jnp.zeros_like(dv)
    for cp in copies:
        cp.wait()

    def step(i, carry):
        slot, row = locate(tab, i)
        here = pl.ds(row, BLOCK)
        q = stack_heads(buf[slot, here, : 2 * BLOCK])
        gated = stack_heads(ga[slot, here, :]).astype(F32)
        grad = stack_heads(dg[slot, here, :]).astype(F32)
        gate = gate_column(buf, slot, row)
        grad_gate = jnp.sum(grad * gated, axis=-1, keepdims=True) * (1.0 - gate)
        grad_low = (grad * gate).astype(LOW)
        q_t = q.astype(F32).T.astype(LOW)
        grad_t = (grad * gate).T.astype(LOW)
        runs = key_pieces(tab, i, pieces)
        weights = []
        total = jnp.zeros((2 * BLOCK, 1), F32)
        for ks, kr, size, keep in runs:
            key = buf[ks, pl.ds(kr, size), 2 * BLOCK : 3 * BLOCK]
            p = keep(jnp.exp2(mm_t(q, key) * factor))
            total = total + jnp.sum(p, axis=-1, keepdims=True)
            weights.append(p)
        inverse = 1.0 / total
        delta = jnp.zeros((2 * BLOCK, 1), F32)
        grad_probs = []
        for (ks, kr, size, keep), p in zip(runs, weights):
            val = buf[ks, pl.ds(kr, size), 3 * BLOCK : 4 * BLOCK]
            grad_p = mm_t(grad_low, val)
            delta = delta + jnp.sum(p * grad_p, axis=-1, keepdims=True)
            grad_probs.append(grad_p)
        delta = delta * inverse
        grad_q = jnp.zeros((2 * BLOCK, BLOCK), F32)
        for (ks, kr, size, keep), p, grad_p in zip(runs, weights, grad_probs):
            key = buf[ks, pl.ds(kr, size), 2 * BLOCK : 3 * BLOCK]
            probs = p * inverse
            grad_s = (probs * (grad_p - delta)).astype(LOW)
            grad_q = grad_q + mm(grad_s, key)
            dk[ks, :, pl.ds(kr, size)] += mm(q_t, grad_s)
            dv[ks, :, pl.ds(kr, size)] += mm(grad_t, probs.astype(LOW))
        grad_q = (grad_q * scale).astype(LOW)
        held[slot, here, :BLOCK] = grad_q[:BLOCK]
        held[slot, here, BLOCK : 2 * BLOCK] = grad_q[BLOCK:]
        lane = lax.broadcasted_iota(jnp.int32, (BLOCK, BLOCK), 1) - jnp.where(slot == 0, 0, 4)
        lanes = jnp.where(lane == 0, grad_gate[:BLOCK], jnp.where(lane == 1, grad_gate[BLOCK:], 0.0))
        held[slot, here, 4 * BLOCK :] = lanes.astype(LOW)
        return carry

    lax.fori_loop(0, blocks, step, 0)

    def finish(i, carry):
        slot, row = locate(tab, i)
        here = pl.ds(row, BLOCK)
        held[slot, here, 2 * BLOCK : 3 * BLOCK] = (dk[slot, :, here].T * scale).astype(LOW)
        held[slot, here, 3 * BLOCK : 4 * BLOCK] = dv[slot, :, here].T.astype(LOW)
        return carry

    lax.fori_loop(0, blocks, finish, 0)
    copies = [
        pltpu.make_async_copy(held.at[0], out_own, sem.at[0]),
        pltpu.make_async_copy(held.at[1], out_sis, sem.at[1]),
    ]
    for cp in copies:
        cp.start()
    for cp in copies:
        cp.wait()


def join_kernel(*refs):
    pieces, weights = refs[:8], refs[8:16]
    tok, gain, middle, hb = refs[16:]
    acc = tok[...].astype(F32)
    for g, w in zip(pieces, weights):
        acc = acc + mm(g[...], w[...])

    @pl.when(pl.program_id(0) == 0)
    def _():
        middle[...] = acc

    hb[...] = (acc * lax.rsqrt(jnp.mean(acc * acc, -1, keepdims=True) + EPSILON) * gain[...]).astype(LOW)


def units_kernel(hb, cot, w_gate, w_up, w_down, mixed, d_gate, d_up):
    gate = mm(hb[...], w_gate[...])
    up = mm(hb[...], w_up[...])
    d_mixed = mm_t(cot[...], w_down[...])
    sig = jax.nn.sigmoid(gate)
    act = gate * sig
    mixed[...] = (act * up).astype(LOW)
    d_gate[...] = (d_mixed * up * sig * (1.0 + gate * (1.0 - sig))).astype(LOW)
    d_up[...] = (d_mixed * act).astype(LOW)


def spread(value, own, send_y, send_x, keep_a, keep_b):
    step = pl.program_id(0)
    half = value.shape[1] // 2
    value = value.astype(LOW)

    @pl.when(step == 0)
    def _():
        send_y[0] = value[:, :half]
        send_x[0] = value[:, half:]

    @pl.when(step == 1)
    def _():
        send_y[0] = value[:, :half]
        keep_b[...] = value[:, half:]

    @pl.when(step == 2)
    def _():
        keep_a[...] = value[:, :half]
        send_x[0] = value[:, half:]

    @pl.when(step == 3)
    def _():
        own[...] = value


def step_block(s):
    return jnp.where(s == 0, 3, jnp.where(s == 3, 0, s))


def spread_outs(rows, width):
    half = width // 2
    return [
        ((rows, width), LOW, (rows, width), lambda s: (0, 0)),
        ((2, rows, half), LOW, (1, rows, half), lambda s: (jnp.where(s == 0, 1, 0), 0, 0)),
        ((2, rows, half), LOW, (1, rows, half), lambda s: (jnp.where(s <= 1, 1, 0), 0, 0)),
        ((rows, half), LOW, (rows, half), lambda s: (0, 0)),
        ((rows, half), LOW, (rows, half), lambda s: (0, 0)),
    ]


def grad_hb_kernel(*refs):
    grads, weights, (hb, own, send_y, send_x, keep_a, keep_b, total) = refs[:4], refs[4:8], refs[8:]
    acc = mm_t(grads[0][...], weights[0][...])
    for g, w in zip(grads[1:], weights[1:]):
        acc = acc + mm_t(g[...], w[...])

    @pl.when(pl.program_id(0) == 0)
    def _():
        total[...] = jnp.zeros_like(total)

    total[...] += jnp.sum(acc * hb[...].astype(F32), axis=0, keepdims=True)
    spread(acc, own, send_y, send_x, keep_a, keep_b)


def down_kernel(m_own, m_sis, w_own, w_sis, own, send_y, send_x, keep_a, keep_b):
    spread(mm(m_own[...], w_own[...]) + mm(m_sis[...], w_sis[...]), own, send_y, send_x, keep_a, keep_b)


def gathered(own, from_y, from_x, last_a, last_b):
    half = own.shape[1] // 2
    left = own[:, :half].astype(F32) + from_y[0].astype(F32) + last_a[...].astype(F32)
    right = own[:, half:].astype(F32) + from_x[0].astype(F32) + last_b[...].astype(F32)
    return jnp.concatenate([left, right], axis=1)


def norm_back(value, gain, incoming):
    r = lax.rsqrt(jnp.mean(value * value, -1, keepdims=True) + EPSILON)
    hat = value * r
    t = incoming * gain
    return r * (t - hat * jnp.mean(t * hat, -1, keepdims=True))


def turn_kernel(own, from_y, from_x, last_a, last_b, middle, cot, gain, *refs):
    weights, (d_middle, attn_a, attn_b, g_own, g_y, g_yd, g_x, g_xd) = refs[:8], refs[8:]
    incoming = gathered(own[...], from_y, from_x, last_a, last_b)
    grad = cot[...].astype(F32) + norm_back(middle[...], gain[...], incoming)
    d_middle[...] = grad
    low = grad.astype(LOW)
    half = low.shape[1] // 2
    attn_a[...] = low[:, :half]
    attn_b[...] = low[:, half:]
    width = weights[0].shape[0]
    for n, (ref, at) in enumerate(
        [(g_own, 0), (g_own, 1), (g_y, 0), (g_y, 1), (g_x, 0), (g_x, 1), (g_xd, 0), (g_yd, 0)]
    ):
        ref[:, at * width : (at + 1) * width] = mm_t(low, weights[n][...]).astype(LOW)


def heads_back_kernel(
    dp_own, dp_sis, lin_own, lin_sis, h, w_own, w_sis, w_gates, cos, sin, qg, kg,
    own, send_y, send_x, keep_a, keep_b, dl_own, dl_sis, dl_gate, q_sum, k_sum, total,
):
    step = pl.program_id(0)

    @pl.when(step == 0)
    def _():
        q_sum[...] = jnp.zeros_like(q_sum)
        k_sum[...] = jnp.zeros_like(k_sum)
        total[...] = jnp.zeros_like(total)

    c, s = cos[...], sin[...]
    for dp, lin, dl in ((dp_own, lin_own, dl_own), (dp_sis, lin_sis, dl_sis)):
        for a in range(3):
            at = slice(a * BLOCK, (a + 1) * BLOCK)
            w = dp[:, at].astype(F32)
            n = w * c - pltpu.roll(w, BLOCK // 2, 1) * s
            u = lin[:, at]
            r = lax.rsqrt(jnp.mean(u * u, -1, keepdims=True) + EPSILON)
            hat = u * r
            into = q_sum if a < 2 else k_sum
            into[...] += jnp.sum(n * hat, axis=0, keepdims=True)
            t = n * (qg if a < 2 else kg)[...]
            dl[:, at] = (r * (t - hat * jnp.mean(t * hat, -1, keepdims=True))).astype(LOW)
        dl[:, 3 * BLOCK :] = dp[:, 3 * BLOCK : 4 * BLOCK]
    gates = dp_own[:, 4 * BLOCK :] + dp_sis[:, 4 * BLOCK :]
    dl_gate[...] = gates
    acc = mm_t(dl_own[...], w_own[...]) + mm_t(dl_sis[...], w_sis[...]) + mm(gates, w_gates[...])
    total[...] += jnp.sum(acc * h[...].astype(F32), axis=0, keepdims=True)
    spread(acc, own, send_y, send_x, keep_a, keep_b)


def last_kernel(own, from_y, from_x, last_a, last_b, tok, gain, d_middle, out, out_low):
    incoming = gathered(own[...], from_y, from_x, last_a, last_b)
    grad = d_middle[...] + norm_back(tok[...].astype(F32), gain[...], incoming)
    low = grad.astype(LOW)
    out_low[...] = low
    out[...] = low.astype(F32)


def place_kernel(axis, parts, idx, *refs):
    blocks, outs = refs[:4], refs[4:]
    turn = jnp.bitwise_xor(pl.program_id(0), idx[0])
    for n in range(4):

        @pl.when(turn == n)
        def _(n=n):
            for (lo, hi), out in zip(parts, outs):
                out[...] = blocks[n][:, lo:hi].astype(F32) if axis else blocks[n][...].astype(F32)


def line_gather(piece, z, axis, first=None):
    right = [(0, 1), (1, 2), (2, 3)]
    left = [(1, 0), (2, 1), (3, 2)]
    if first is not None:
        piece = after(piece, *first)
    r1 = lax.ppermute(piece, "wide", right)
    l1 = lax.ppermute(piece, "wide", left)
    r2 = lax.ppermute(r1, "wide", right[1:])
    l2 = lax.ppermute(l1, "wide", left[:2])
    r3 = lax.ppermute(r2, "wide", right[2:])
    l3 = lax.ppermute(l2, "wide", left[:1])
    s1 = jnp.where(z >= 1, r1, l3)
    s2 = jnp.where(z >= 2, r2, l2)
    s3 = jnp.where(z == 3, r3, l1)
    size = piece.shape[axis]
    shape = list(piece.shape)
    shape[axis] = 4 * size
    full = jnp.zeros(shape, piece.dtype)
    for k, part in enumerate((piece, s3, s2, s1)):
        full = lax.dynamic_update_slice_in_dim(full, part, ((z + k) % 4) * size, axis)
    return full, (r1, l1)


def line_scatter(whole, z, axis):
    size = whole.shape[axis] // 4
    right = [(0, 1), (1, 2), (2, 3)]
    left = [(1, 0), (2, 1), (3, 2)]

    def part(offset):
        return lax.dynamic_slice_in_dim(whole, ((z + offset + 4) % 4) * size, size, axis)

    def plus(a, b):
        return (a.astype(F32) + b.astype(F32)).astype(LOW)

    a = lax.ppermute(part(3), "wide", right[:1])
    b = lax.ppermute(part(-3), "wide", left[2:])
    a = lax.ppermute(plus(part(2), a), "wide", right[:2])
    b = lax.ppermute(plus(part(-2), b), "wide", left[1:])
    a = lax.ppermute(plus(part(1), a), "wide", right)
    b = lax.ppermute(plus(part(-1), b), "wide", left)
    return (part(0).astype(F32) + a.astype(F32) + b.astype(F32)).astype(LOW)


def four(a, b):
    x_a, y_b = over_x(a), over_y(b)
    y_a, x_b = over_y(a), over_x(b)
    d_a, d_b = over_y(x_a), over_x(y_b)
    return [(a, b), (y_a, y_b), (x_a, x_b), (d_a, d_b)]


def plane_sum(own, send_y, send_x, keep_a, keep_b):
    from_y = over_y(send_y)
    from_x = over_x(send_x)
    last_a = over_x((keep_a.astype(F32) + from_y[1].astype(F32)).astype(LOW))
    last_b = over_y((keep_b.astype(F32) + from_x[1].astype(F32)).astype(LOW))
    return own, from_y, from_x, last_a, last_b


def plane_ins(pieces):
    own, from_y, from_x, last_a, last_b = pieces
    rows, width = own.shape
    half = width // 2
    return [
        (own, (rows, width), lambda s: (0, 0)),
        (from_y, (1, rows, half), lambda s: (0, 0, 0)),
        (from_x, (1, rows, half), lambda s: (0, 0, 0)),
        (last_a, (rows, half), lambda s: (0, 0)),
        (last_b, (rows, half), lambda s: (0, 0)),
    ]


def place(shard, idx, axis, parts):
    from_core, from_x = over_core(shard), over_x(shard)
    blocks = [shard, from_core, from_x, over_core(from_x)]
    rows, width = shard.shape
    outs = []
    for lo, hi in parts:
        if axis:
            outs.append(((rows, 4 * (hi - lo)), F32, (rows, hi - lo), lambda p: (0, p)))
        else:
            outs.append(((4 * rows, width), F32, (rows, width), lambda p: (p, 0)))
    return call(
        functools.partial(place_kernel, axis, parts),
        (4,),
        [(idx, None, pltpu.SMEM)] + [(b, (rows, width), None) for b in blocks],
        outs,
        0,
        name="place",
    )


def total_over(values, axes):
    for move in axes:
        values = values + move(values)
    return values


def visit_table(segment_of, parent_of, valid, x, core, y, rows):
    per = rows // BLOCK
    half = per // 2
    i = jnp.arange(4 * per, dtype=jnp.int32)
    seg, live = segment_of[::BLOCK], valid[::BLOCK]
    context = i // per
    slot = (context % 2) ^ core
    block = ((context // 2) ^ x) * 2 + ((i % per) // half ^ y)
    row = (block * half + i % half) * BLOCK
    trunk = seg[0]
    parent = jnp.sum(
        jnp.where(seg[:, None] == jnp.arange(parent_of.shape[0])[None, :], parent_of[None, :], 0), axis=1
    )
    has = (live > 0) & (seg != trunk) & (parent != trunk)
    match = (live[None, :] > 0) & (seg[None, :] == parent[:, None])
    where = jnp.min(jnp.where(match, i[None, :], 4 * per - 1), axis=1)
    pick = where[:, None] == i[None, :]
    p_slot = jnp.sum(jnp.where(pick, slot[None, :], 0), axis=1)
    p_row = jnp.sum(jnp.where(pick, row[None, :], 0), axis=1)
    limit = jnp.where(live > 0, jnp.where(seg == trunk, i * BLOCK, TRUNK), 0)
    return jnp.stack([slot, row, limit, p_slot, p_row, has.astype(jnp.int32), live]).astype(jnp.int32)


def plane_shards(
    tokens, segment_of, parent_of, valid, positions, g_attn, w_q, key_projection, value_projection, w_g,
    q_gain, k_gain, w_o, g_mlp, w_gate, w_up, w_down, cotangent,
):
    rows, width = tokens.shape
    part = rows // 2
    z, c, y = lax.axis_index("wide"), lax.axis_index("context"), lax.axis_index("tensor")
    x, core = c // 2, c % 2
    scale = BLOCK ** (-0.5)
    factor = scale * 1.4426950408889634

    def cut(w, axis):
        size = w.shape[axis] // 4
        return lax.dynamic_slice_in_dim(w, c * size, size, axis)

    depth = w_q.shape[0]
    small = jnp.concatenate(
        [g_attn[None, :], g_mlp[None, :], w_g.T, jnp.zeros((6, depth), LOW)], axis=0
    )
    small_full, small_step = line_gather(small, z, 1)
    attn_gain = small_full[0:1].astype(F32)
    mlp_gain = small_full[1:2].astype(F32)
    gates_t = small_full[2:10]
    own_rows = lax.dynamic_slice_in_dim(gates_t, 2 * c, 2, 0)
    sis_rows = lax.dynamic_slice_in_dim(gates_t, 2 * (c ^ 1), 2, 0)
    gate_rows = jnp.concatenate(
        [own_rows, own_rows, sis_rows, sis_rows, jnp.zeros((BLOCK - 8, width), LOW)], axis=0
    )

    qkv = jnp.concatenate([cut(w_q, 1), cut(key_projection, 1), cut(value_projection, 1)], axis=1)
    qkv_own, st = line_gather(qkv, z, 0)
    wo_own, st = line_gather(cut(w_o, 0), z, 1, st)
    wg_own, st = line_gather(cut(w_gate, 1), z, 0, st)
    wu_own, st = line_gather(cut(w_up, 1), z, 0, st)
    wd_own, st = line_gather(cut(w_down, 0), z, 1, st)
    qkv_sis = over_core(qkv_own)
    wo_sis = over_core(wo_own)
    wg_sis, wu_sis, wd_sis = over_core(wg_own), over_core(wu_own), over_core(wd_own)

    def halves(v):
        return (
            lax.dynamic_slice_in_dim(v, y * part, part, 0),
            lax.dynamic_slice_in_dim(v, (1 - y) * part, part, 0),
        )

    tok0, tok1 = halves(tokens)
    cut2 = part // 2
    t2 = [over_x(tok0[:cut2]), over_x(tok0[cut2:])]
    t3 = [over_y(v) for v in t2]
    tok_near = jnp.concatenate([tok0, tok1], axis=0)
    tok_far = jnp.concatenate(t2 + t3, axis=0)
    cot0, cot1 = halves(cotangent)
    cot_first = after(cot0, *t3)
    c2 = [over_x(cot_first[:cut2]), over_x(cot_first[cut2:])]
    c3 = [over_y(v) for v in c2]
    cot = jnp.concatenate([cot0, cot1] + c2 + c3, axis=0)

    pos = positions.astype(F32).reshape(rows // BLOCK, BLOCK)
    pos_far = over_x(pos)

    def tables(p):
        p0, p1 = halves(p.reshape(rows))
        cosine, sine = rope_tables(jnp.concatenate([p0, p1]), BLOCK)
        sign = jnp.where(jnp.arange(BLOCK) < BLOCK // 2, -1.0, 1.0)
        return cosine, sine * sign

    qg, kg = q_gain.astype(F32)[None, :], k_gain.astype(F32)[None, :]
    near_tables, far_tables = tables(pos), tables(pos_far)
    three, four_, five = 3 * BLOCK, 4 * BLOCK, 5 * BLOCK

    def prep(tok, tab):
        return call(
            prep_kernel,
            (2,),
            [
                (tok, (part, width), lambda s: (s, 0)),
                (attn_gain, (1, width), None),
                (qkv_own, qkv_own.shape, None),
                (qkv_sis, qkv_sis.shape, None),
                (gate_rows, gate_rows.shape, None),
                (tab[0], (part, BLOCK), lambda s: (s, 0)),
                (tab[1], (part, BLOCK), lambda s: (s, 0)),
                (qg, (1, BLOCK), None),
                (kg, (1, BLOCK), None),
            ],
            [
                ((rows, width), LOW, (part, width), lambda s: (s, 0)),
                ((rows, three), F32, (part, three), lambda s: (s, 0)),
                ((rows, three), F32, (part, three), lambda s: (s, 0)),
                ((rows, five), LOW, (part, five), lambda s: (s, 0)),
                ((rows, five), LOW, (part, five), lambda s: (s, 0)),
            ],
            2 * rows * width * 9 * BLOCK,
            name="prep",
        )

    near = prep(tok_near, near_tables)
    far = prep(tok_far, far_tables)
    pk_own = jnp.concatenate([near[3], far[3]], axis=0)
    pk_sis = jnp.concatenate([over_core(near[4]), over_core(far[4])], axis=0)

    tab = visit_table(segment_of, parent_of, valid, x, core, y, rows)
    per = rows // BLOCK
    half = per // 2
    blocks = 4 * per
    pieces = [(f, min(half, TRUNK // BLOCK - f)) for f in range(0, TRUNK // BLOCK, half)]
    all_rows = 2 * rows
    ANY, SMEM, VMEM = pl.ANY, pltpu.SMEM, pltpu.VMEM
    gated_own, gated_out = call(
        functools.partial(attend_kernel, blocks, pieces, factor),
        (1,),
        [(tab, None, SMEM), (pk_own, None, ANY), (pk_sis, None, ANY)],
        [((all_rows, 2 * BLOCK), LOW, None, ANY)] * 2,
        blocks * 4 * 256 * 1280 * 128,
        scratch=[
            VMEM((2, all_rows, five), LOW),
            VMEM((2, all_rows, 2 * BLOCK), LOW),
            pltpu.SemaphoreType.DMA((2,)),
        ],
        name="attend",
    )
    gated_sis = over_core(gated_out)
    gated = four(gated_own, gated_sis)
    wo = four(wo_own, wo_sis)
    tok_all = jnp.concatenate([tok_near, tok_far], axis=0)
    two = 2 * BLOCK
    turns = [0, 1, 2, 3]
    middle, hb = call(
        join_kernel,
        (4,),
        [(g, (part, two), lambda s, t=t: (s ^ t, 0)) for t, pair in zip(turns, gated) for g in pair]
        + [(w, (two, width), None) for pair in wo for w in pair]
        + [(tok_all, (part, width), lambda s: (s, 0)), (mlp_gain, (1, width), None)],
        [
            ((part, width), F32, (part, width), lambda s: (0, 0)),
            ((all_rows, width), LOW, (part, width), lambda s: (s, 0)),
        ],
        2 * all_rows * width * width,
        name="join",
    )

    units = wg_own.shape[1]

    def hidden(wg, wu, wd):
        return call(
            units_kernel,
            (4,),
            [
                (hb, (part, width), lambda s: (s, 0)),
                (cot, (part, width), lambda s: (s, 0)),
                (wg, wg.shape, None),
                (wu, wu.shape, None),
                (wd, wd.shape, None),
            ],
            [((all_rows, units), LOW, (part, units), lambda s: (s, 0))] * 3,
            6 * all_rows * width * units,
            name="units",
        )

    mixed_own, dg_own, du_own = hidden(wg_own, wu_own, wd_own)
    mixed_sis, dg_sis, du_sis = hidden(wg_sis, wu_sis, wd_sis)

    by_block = lambda s: (step_block(s), 0)
    total_spec = ((1, width), F32, (1, width), lambda s: (0, 0))
    *dhb, hb_total = call(
        grad_hb_kernel,
        (4,),
        [(g, (part, units), by_block) for g in (dg_own, du_own, dg_sis, du_sis)]
        + [(w, w.shape, None) for w in (wg_own, wu_own, wg_sis, wu_sis)]
        + [(hb, (part, width), by_block)],
        spread_outs(part, width) + [total_spec],
        8 * all_rows * width * units,
        name="grad_hb",
    )
    dhb = plane_sum(*dhb)

    out_parts = call(
        down_kernel,
        (4,),
        [
            (mixed_own, (part, units), by_block),
            (mixed_sis, (part, units), by_block),
            (wd_own, wd_own.shape, None),
            (wd_sis, wd_sis.shape, None),
        ],
        spread_outs(part, width),
        4 * all_rows * width * units,
        name="down",
    )

    def core_sum(sent, kept):
        return (kept + over_core(sent.astype(LOW)).astype(F32)).astype(LOW)

    gd = core_sum(product_left(mixed_sis, cot), product_left(mixed_own, cot))
    gg = core_sum(product_left(hb, dg_sis), product_left(hb, dg_own))
    gu = core_sum(product_left(hb, du_sis), product_left(hb, du_own))
    gd_shard = line_scatter(gd, z, 1)
    gg_shard = line_scatter(gg, z, 0)
    gu_shard = line_scatter(gu, z, 0)

    flat = [(w, w.shape, None) for pair in wo for w in pair]
    half_w = width // 2
    first = lambda s: (0, 0)
    d_middle, attn_a, attn_b, g_own, g_y, g_yd, g_x, g_xd = call(
        turn_kernel,
        (1,),
        plane_ins(dhb)
        + [
            (middle, (part, width), first),
            (cot, (part, width), first),
            (mlp_gain, (1, width), first),
        ]
        + flat,
        [
            ((part, width), F32, (part, width), first),
            ((part, half_w), LOW, (part, half_w), first),
            ((part, half_w), LOW, (part, half_w), first),
            ((part, 2 * two), LOW, (part, 2 * two), first),
            ((part, 2 * two), LOW, (part, 2 * two), first),
            ((part, two), LOW, (part, two), first),
            ((part, 2 * two), LOW, (part, 2 * two), first),
            ((part, two), LOW, (part, two), first),
        ],
        2 * part * width * width,
        name="turn",
    )
    r_y, r_x = over_y(g_y), over_x(g_x)
    r_xd, r_yd = over_y(over_x(g_xd)), over_x(over_y(g_yd))
    dgated_own = jnp.concatenate([g_own[:, :two], r_y[:, :two], r_x[:, :two], r_xd], axis=0)
    dgated_sis = over_core(jnp.concatenate([g_own[:, two:], r_y[:, two:], r_x[:, two:], r_yd], axis=0))
    dp_own, dp_out = call(
        functools.partial(attend_back_kernel, blocks, pieces, factor, scale),
        (1,),
        [(tab, None, SMEM)]
        + [(v, None, ANY) for v in (pk_own, pk_sis, gated_own, gated_out, dgated_own, dgated_sis)],
        [((all_rows, five), LOW, None, ANY)] * 2,
        blocks * 10 * 256 * 1280 * 128,
        scratch=[
            VMEM((2, all_rows, five), LOW),
            VMEM((2, all_rows, two), LOW),
            VMEM((2, all_rows, two), LOW),
            VMEM((2, all_rows, five), LOW),
            VMEM((2, BLOCK, all_rows), F32),
            VMEM((2, BLOCK, all_rows), F32),
            pltpu.SemaphoreType.DMA((6,)),
        ],
        name="attend_back",
    )
    dp_sis = over_core(dp_out)
    lin_own = jnp.concatenate([near[1], far[1]], axis=0)
    lin_sis = jnp.concatenate([near[2], far[2]], axis=0)
    h = jnp.concatenate([near[0], far[0]], axis=0)
    cos = jnp.concatenate([near_tables[0], far_tables[0]], axis=0)
    sin = jnp.concatenate([near_tables[1], far_tables[1]], axis=0)
    one = ((1, BLOCK), F32, (1, BLOCK), first)
    *dh, dl_own, dl_sis, dl_gate, q_sum, k_sum, h_total = call(
        heads_back_kernel,
        (4,),
        [
            (dp_own, (part, five), by_block),
            (dp_sis, (part, five), by_block),
            (lin_own, (part, three), by_block),
            (lin_sis, (part, three), by_block),
            (h, (part, width), by_block),
            (qkv_own, qkv_own.shape, None),
            (qkv_sis, qkv_sis.shape, None),
            (gate_rows, gate_rows.shape, None),
            (cos, (part, BLOCK), by_block),
            (sin, (part, BLOCK), by_block),
            (qg, (1, BLOCK), None),
            (kg, (1, BLOCK), None),
        ],
        spread_outs(part, width)
        + [
            ((all_rows, four_), LOW, (part, four_), by_block),
            ((all_rows, four_), LOW, (part, four_), by_block),
            ((all_rows, BLOCK), LOW, (part, BLOCK), by_block),
            one,
            one,
            total_spec,
        ],
        2 * all_rows * width * 9 * BLOCK,
        name="heads_back",
    )
    dh = plane_sum(*dh)
    grad_tokens_own, grad_low = call(
        last_kernel,
        (1,),
        plane_ins(dh)
        + [
            (tok0, (part, width), first),
            (attn_gain, (1, width), first),
            (d_middle, (part, width), first),
        ],
        [((part, width), F32, (part, width), first), ((part, width), LOW, (part, width), first)],
        part * width * 16,
        name="last",
    )

    def both_halves(mine, other):
        return jnp.where(
            y == 0, jnp.concatenate([mine, other], axis=0), jnp.concatenate([other, mine], axis=0)
        )

    grad_tokens = both_halves(grad_tokens_own, over_y(grad_low).astype(F32))

    gq = core_sum(product_left(h, dl_sis), product_left(h, dl_own))
    gq_shard = line_scatter(gq, z, 0)
    attn_low = four(attn_a, attn_b)
    order = [attn_low[0], attn_low[1], attn_low[2], attn_low[3]]
    d_attn = jnp.concatenate(
        [jnp.concatenate([a for a, _ in order], axis=0), jnp.concatenate([b for _, b in order], axis=0)], axis=1
    )
    go = core_sum(product_left(gated_sis, d_attn), product_left(gated_own, d_attn))
    go_shard = line_scatter(go, z, 1)

    sums = plane_sum(*out_parts)
    out_own = (middle + gathered(*sums)).astype(LOW)
    layer_out = both_halves(out_own, over_y(out_own))

    gate_grad = product_left(dl_gate, h)
    rows_of = jnp.arange(8, dtype=jnp.int32)[:, None]
    gate_rows_grad = jnp.zeros((8, width), F32)
    for n, row in ((0, 2 * c), (1, 2 * c + 1), (4, 2 * (c ^ 1)), (5, 2 * (c ^ 1) + 1)):
        gate_rows_grad = gate_rows_grad + jnp.where(rows_of == row, gate_grad[n : n + 1], 0.0)
    gains = jnp.concatenate(
        [
            h_total / attn_gain,
            hb_total / mlp_gain,
            jnp.concatenate([q_sum, k_sum, jnp.zeros((1, width - two), F32)], axis=1),
            jnp.zeros((5, width), F32),
        ],
        axis=0,
    )
    gains = gains + over_y(gains)
    packed = jnp.concatenate([gate_rows_grad, gains], axis=0)
    packed = packed + over_core(packed)
    packed = packed + over_x(packed)
    packed = packed + lax.ppermute(packed, "wide", [(0, 1), (1, 0), (2, 3), (3, 2)])
    packed = packed + lax.ppermute(packed, "wide", [(0, 2), (2, 0), (1, 3), (3, 1)])
    mine = lax.dynamic_slice_in_dim(packed, z * depth, depth, 1)

    idx = c.reshape(1).astype(jnp.int32)
    whole_units = [(0, units)]
    (final_gate,) = place(gg_shard, idx, 1, whole_units)
    (final_up,) = place(gu_shard, idx, 1, whole_units)
    (final_down,) = place(gd_shard, idx, 0, [(0, depth)])
    (final_out,) = place(go_shard, idx, 0, [(0, depth)])
    final_q, final_k, final_v = place(gq_shard, idx, 1, [(0, two), (two, three), (three, four_)])
    return (
        layer_out,
        grad_tokens,
        mine[8],
        final_q,
        final_k,
        final_v,
        mine[:8].T,
        packed[10, :BLOCK],
        packed[10, BLOCK:two],
        final_out,
        mine[9],
        final_gate,
        final_up,
        final_down,
    )


def solution(mesh):
    placed = (
        P(("wide", "context"), None),
        P("wide"),
        P("wide"),
        P("wide"),
        P(("wide", "context")),
        P("wide"),
        P("wide", "tensor"),
        P("wide", "tensor"),
        P("wide", "tensor"),
        P("wide", "tensor"),
        P(),
        P(),
        P("tensor", "wide"),
        P("wide"),
        P("wide", "tensor"),
        P("wide", "tensor"),
        P("tensor", "wide"),
        P(("wide", "context"), None),
    )
    in_planes = mesh.shape["wide"] == 4 and mesh.shape["context"] == 4 and mesh.shape["tensor"] == 2
    return jax.shard_map(
        plane_shards if in_planes else shards,
        mesh=mesh,
        in_specs=placed,
        out_specs=(
            P(("wide", "context"), None),
            P(("wide", "context"), None),
            P("wide"),
            P("wide", "tensor"),
            P("wide", "tensor"),
            P("wide", "tensor"),
            P("wide", "tensor"),
            P(),
            P(),
            P("tensor", "wide"),
            P("wide"),
            P("wide", "tensor"),
            P("wide", "tensor"),
            P("tensor", "wide"),
        ),
        check_vma=False,
    )
```
